1024 devices in a mesh: section: 4 (over x), seq: 256 (over z, y, core).
Axes of the slice: x: 4, y: 8, z: 16, core: 2. Of those that a mesh axis runs over, the one named last changes fastest.
Arguments:
- queries: bfloat16 [4, 32768, 3072], P('section', 'seq'), may hold values from -60 to 60
- packed_key_value: bfloat16 [4, 32768, 1024], P('section', 'seq'), may hold values from -6 to 6
- incoming: bfloat16 [4, 32768, 3072], P('section', 'seq'), may hold values from -6 to 6
- loss_grad: bfloat16 [32768, 3072], P('seq'), may hold values from -6 to 6
- global_blocks: int32 [4, 2], P('section'), may hold values from 0 to 511
- random_blocks: int32 [4, 512, 4, 3], P('section'), may hold values from 0 to 511, as said below
Outputs:
- d_queries: bfloat16 [4, 32768, 3072], P('section', 'seq')
- d_key_value: bfloat16 [4, 32768, 1024], P('section', 'seq')
The draws below stay inside these ranges and needn't reach their ends.
Inputs may be any that keep to these rules, and one draw needn't show every extreme that they name: `random_blocks`: the random blocks of a query block lie among the blocks held by the seq index that holds the query block and the indices just before and after it.
All inputs are finite; a program needn't handle non-finite values.
Results may differ from the reference program's by a relative error of at most 0.006.
Values may be sent and summed in bfloat16 or wider, within the bound.
A program may use at most 32 MiB of HBM per device.

```python
import math
import jax
import jax.numpy as jnp
from jax import lax

HQ = 24
KEY_HEADS = 4
HEAD_SIZE = 128
BLOCK_TOKENS = 64
GLOBAL_BLOCKS = 2
RANDOM_BLOCKS = 3
TOK_DEV = 128
GROUP_HEADS = 6
SEQUENCE_TOKENS = 32768
N_SECTION = 4


def base_pairs(key):
    sub_key = jax.random.fold_in(key, 101)
    complete_shape = (N_SECTION, SEQUENCE_TOKENS, 2 * KEY_HEADS * HEAD_SIZE)
    block_pairs = jnp.clip(jax.random.normal(sub_key, complete_shape, jnp.float32), -6.0, 6.0)
    return block_pairs


def draw_packed_key_value(key, part):
    return base_pairs(key).astype(jnp.bfloat16)


def draw_queries(key, part):
    complete_shape = (N_SECTION, SEQUENCE_TOKENS, HQ * HEAD_SIZE)
    sub_key = jax.random.fold_in(key, 202)
    values_out = jnp.clip(jax.random.normal(sub_key, complete_shape, jnp.float32), -6.0, 6.0)
    return values_out.astype(jnp.bfloat16)


def draw_random_blocks(key, part):
    local_block_count = TOK_DEV // BLOCK_TOKENS
    every_block = SEQUENCE_TOKENS // BLOCK_TOKENS
    seq_count = SEQUENCE_TOKENS // TOK_DEV
    device_ids = jnp.arange(every_block, dtype=jnp.int32) // local_block_count
    lower = jnp.maximum(device_ids - 1, 0) * local_block_count
    upper = jnp.minimum(device_ids + 2, seq_count) * local_block_count
    random_integers = jax.random.randint(jax.random.fold_in(key, 404), (N_SECTION, every_block, KEY_HEADS, RANDOM_BLOCKS), 0, 1 << 20)
    spans = (upper - lower)[None, :, None, None]
    return (lower[None, :, None, None] + random_integers % spans).astype(jnp.int32)


def plant(result, key, low, top_value):
    longest = result.shape.index(max(result.shape))
    spots = []
    for shift in (0, 1):
        where = [jax.random.randint(jax.random.fold_in(key, axis), (), 0, length) for axis, length in enumerate(result.shape)]
        where[longest] = (where[longest] + shift) % result.shape[longest]
        spots.append(tuple(where))
    return result.at[spots[0]].set(low).at[spots[1]].set(top_value)


def level_of(stream_key, extent, shards, least, largest):
    factor_of = 1.0
    for axis_at, blocks in shards:
        steps = jax.random.uniform(jax.random.fold_in(jax.random.fold_in(stream_key, 6), axis_at), (blocks,), jnp.float32, least / len(shards), largest / len(shards))
        factor_of = factor_of * jnp.repeat(jnp.exp(steps), extent[axis_at] // blocks).reshape((-1,) + (1,) * (len(extent) - 1 - axis_at))
    return factor_of


def gaussian(stream_key, shape, deviation, limit, shards=(), kind=jnp.bfloat16):
    gain = level_of(stream_key, shape, shards, -0.22, 0.18) if shards else 1.0
    array = jax.random.normal(stream_key, shape, jnp.float32) * deviation * gain
    return jnp.minimum(jnp.maximum(array, -limit), limit).astype(kind)


def setup_inputs(seed: int = 0) -> dict:
    key_list = jax.random.split(jax.random.key(seed), 7)
    queries = draw_queries(jax.random.fold_in(key_list[6], 71), 0)
    packed_key_value = draw_packed_key_value(jax.random.fold_in(key_list[6], 71), 0)
    incoming = gaussian(key_list[2], (N_SECTION, SEQUENCE_TOKENS, HQ * HEAD_SIZE), 1.0, 6.0, ((0, 4), (1, 256)))
    loss_grad = gaussian(key_list[3], (SEQUENCE_TOKENS, HQ * HEAD_SIZE), 1.0, 6.0, ((0, 256),))
    global_blocks = plant(jax.random.randint(key_list[4], (N_SECTION, GLOBAL_BLOCKS), 0, SEQUENCE_TOKENS // BLOCK_TOKENS), jax.random.fold_in(key_list[4], 1), 0, (SEQUENCE_TOKENS // BLOCK_TOKENS) - 1).astype(jnp.int32)
    random_blocks = draw_random_blocks(jax.random.fold_in(key_list[6], 71), 0)
    return {"queries": queries, "packed_key_value": packed_key_value, "incoming": incoming, "loss_grad": loss_grad, "global_blocks": global_blocks, "random_blocks": random_blocks}


def section_grads(section_args):
    queries, packed_key_value, output_gradient, global_block_index, random_block_index = section_args
    score_scale = 1.0 / math.sqrt(HEAD_SIZE)
    every_block = SEQUENCE_TOKENS // BLOCK_TOKENS
    block_ids = jnp.arange(every_block, dtype=jnp.int32)
    window_blocks = block_ids[:, None] + jnp.arange(-1, 2, dtype=jnp.int32)[None, :]
    usable = jnp.concatenate([(window_blocks >= 0) & (window_blocks < every_block), jnp.ones((every_block, GLOBAL_BLOCKS + RANDOM_BLOCKS), dtype=bool)], 1)
    window_blocks = jnp.clip(window_blocks, 0, every_block - 1).astype(jnp.int32)
    global_key_tile = jnp.broadcast_to(global_block_index.astype(jnp.int32)[None, None, :], (KEY_HEADS, every_block, GLOBAL_BLOCKS))
    key_block_index = jnp.concatenate([jnp.broadcast_to(window_blocks[None], (KEY_HEADS, every_block, 3)), global_key_tile, jnp.transpose(random_block_index, (1, 0, 2)).astype(jnp.int32)], 2)
    key_mask = jnp.repeat(usable, BLOCK_TOKENS, axis=1)
    query_group_rows = queries.reshape(every_block, BLOCK_TOKENS, KEY_HEADS, GROUP_HEADS, HEAD_SIZE).transpose(2, 0, 1, 3, 4)
    gradient_group_rows = output_gradient.reshape(every_block, BLOCK_TOKENS, KEY_HEADS, GROUP_HEADS, HEAD_SIZE).transpose(2, 0, 1, 3, 4)
    paired_groups = packed_key_value.reshape(every_block, BLOCK_TOKENS, 2, KEY_HEADS, HEAD_SIZE).transpose(3, 0, 1, 2, 4)

    def one_group(group_args):
        index_g, query_grouped, gradient_grouped, pairs_g = group_args
        selected = pairs_g[index_g]
        key_row_block = selected[:, :, :, 0].reshape(every_block, -1, HEAD_SIZE).astype(jnp.float32)
        value_row_block = selected[:, :, :, 1].reshape(every_block, -1, HEAD_SIZE).astype(jnp.float32)
        query_wide = query_grouped.astype(jnp.float32)
        gradient_wide = gradient_grouped.astype(jnp.float32)
        logit_scores = jnp.einsum('elmi,eti->emlt', query_wide, key_row_block) * score_scale
        logit_scores = jnp.where(key_mask[:, None, None, :], logit_scores, -1e+30)
        row_max = lax.optimization_barrier(jnp.max(logit_scores, axis=-1, keepdims=True))
        weights_raw = jnp.exp(logit_scores - row_max)
        probs = weights_raw / lax.optimization_barrier(jnp.sum(weights_raw, axis=-1, keepdims=True))
        probability_lowbits = probs.astype(jnp.bfloat16)
        probability_gradient = jnp.einsum('elmi,eti->emlt', gradient_wide, value_row_block)
        row_delta = lax.optimization_barrier(jnp.sum(probs * probability_gradient, axis=-1, keepdims=True))
        score_gradient = (probs * (probability_gradient - row_delta) * score_scale).astype(jnp.bfloat16)
        scores_wide = score_gradient.astype(jnp.float32)
        query_gradient = jnp.einsum('yzmu,yup->ymzp', scores_wide, key_row_block)
        key_gradient = jnp.einsum('xapt,xpag->xtg', scores_wide, query_wide)
        value_gradient = jnp.einsum('xapt,xpag->xtg', probability_lowbits.astype(jnp.float32), gradient_wide)
        paired = jnp.stack([key_gradient, value_gradient], 2).reshape(-1, BLOCK_TOKENS, 2, HEAD_SIZE)
        summed = jnp.zeros((every_block, BLOCK_TOKENS, 2, HEAD_SIZE), jnp.float32).at[index_g.reshape(-1)].add(paired)
        return (query_gradient, summed)
    grad_query_all, reduced_total = lax.map(one_group, (key_block_index, query_group_rows, gradient_group_rows, paired_groups))
    d_q = grad_query_all.transpose(1, 2, 0, 3, 4).reshape(SEQUENCE_TOKENS, HQ * HEAD_SIZE).astype(jnp.bfloat16)
    key_value_gradient = reduced_total.transpose(1, 2, 3, 0, 4).reshape(SEQUENCE_TOKENS, 2 * KEY_HEADS * HEAD_SIZE).astype(jnp.bfloat16)
    return (d_q, key_value_gradient)

def reference(queries, packed_key_value, incoming, loss_grad, global_blocks, random_blocks):
    d_out_all = jnp.concatenate([incoming[1:], loss_grad[None]], 0)
    d_queries, d_key_value = lax.map(section_grads, (queries, packed_key_value, d_out_all, global_blocks, random_blocks))
    return (d_queries, d_key_value)
```

```python
import functools
import math

import jax
import jax.numpy as jnp
from jax import lax
from jax.experimental import pallas as pl
from jax.experimental.pallas import tpu as pltpu
from jax.sharding import PartitionSpec as P

HQ = 24
KEY_HEADS = 4
HEAD = 128
BLOCK = 64
GROUP = 6
TOK = 128
GROUP_COLS = GROUP * HEAD
KEYS = 3 * TOK + 2 * BLOCK
HALVES = 2
PER_HALF = KEY_HEADS // HALVES
MESH = pl.DeviceIdType.MESH
F32 = jnp.float32
BF16 = jnp.bfloat16
SCALE = 1.0 / math.sqrt(HEAD)
LOG2E = math.log2(math.e)


def kernel(
    n_sec, plane, nz,
    q_hbm, kv_hbm, inc_hbm, loss_hbm, gb_ref, rb_ref,
    dq_hbm, dkv_hbm,
    qv, dout, kvo, kvh, bias, kall, vall, kallt,
    g1src, r1a, r1b, r2a, r2b, gkv,
    acc, own, hgs, hgr, g2src, g2r1, g2r2, g2f, dqv, dkvv,
    in_sem, loss_sem, out_sem,
    sh_s, sh_r, ha_s, ha_r, hg_s, hg_r, pl_s, pl_r,
):
    n_seq = plane * nz
    r1, r2 = (r1a, r1b), (r2a, r2b)
    ch = 4 * BLOCK // plane
    rows = min(ch, BLOCK)
    s = lax.axis_index("section")
    q = lax.axis_index("seq")
    z = q // plane
    yc = q % plane
    right = (s, lax.rem(q + 1, n_seq))
    left = (s, lax.rem(q + n_seq - 1, n_seq))
    back = (lax.rem(s + n_sec - 1, n_sec), q)
    ahead = (lax.rem(s + 1, n_sec), q)

    def plane_peer(i):
        k = lax.rem(yc + i, plane)
        return k, (s, z * plane + k)

    def z_peer(i):
        k = lax.rem(z + i, nz)
        return k, (s, k * plane + yc)

    barrier = pltpu.get_barrier_semaphore()
    for peer in (right, left, back, ahead):
        pl.semaphore_signal(barrier, inc=1, device_id=peer, device_id_type=MESH)

    @pl.loop(1, plane)
    def _(i):
        pl.semaphore_signal(barrier, inc=1, device_id=plane_peer(i)[1], device_id_type=MESH)

    @pl.loop(1, nz)
    def _(i):
        pl.semaphore_signal(barrier, inc=1, device_id=z_peer(i)[1], device_id_type=MESH)

    load_kv = pltpu.make_async_copy(kv_hbm.at[0], kvo, in_sem.at[0])
    load_q = pltpu.make_async_copy(q_hbm.at[0], qv, in_sem.at[1])
    load_kv.start()
    load_q.start()

    def cols(g):
        return pl.ds(pl.multiple_of(g * GROUP_COLS, GROUP_COLS), GROUP_COLS)

    def loss_copy(g):
        return pltpu.make_async_copy(loss_hbm.at[:, cols(g)], dout.at[g], loss_sem.at[g])

    @pl.when(s == n_sec - 1)
    def _():
        for g in range(KEY_HEADS):
            loss_copy(g).start()

    pl.semaphore_wait(barrier, 4 + plane - 1 + nz - 1)

    def shift(g):
        return pltpu.make_async_remote_copy(
            inc_hbm.at[0, :, cols(g)], dout.at[g], sh_s.at[g], sh_r.at[g], back, MESH
        )

    @pl.when(s > 0)
    def _():
        for g in range(KEY_HEADS):
            shift(g).start()

    load_kv.wait()
    for j in range(2):
        high = lax.rem(gb_ref[0, j], 2) == 1
        block = jnp.where(high, kvo[BLOCK:, :], kvo[:BLOCK, :])
        for part in range(2):
            for g in range(KEY_HEADS):
                col = part * KEY_HEADS * HEAD + g * HEAD
                for i in range(BLOCK // rows):
                    at = part * 2 * BLOCK + j * BLOCK + i * rows
                    g1src[g // PER_HALF, at // ch, g % PER_HALF, at % ch : at % ch + rows, :] = block[
                        i * rows : (i + 1) * rows, col : col + HEAD
                    ]

    def all_of(buf, count, sem):
        return pltpu.make_async_copy(buf.at[pl.ds(0, count)], buf.at[pl.ds(0, count)], sem)

    def plane_scatter(src, dst, row):
        @pl.loop(1, plane)
        def _(i):
            k, peer = plane_peer(i)
            pltpu.make_async_remote_copy(
                src.at[k], dst.at[yc], pl_s.at[row], pl_r.at[row], peer, MESH
            ).start()

    def plane_gather(buf, row):
        @pl.loop(1, plane)
        def _(i):
            _, peer = plane_peer(i)
            pltpu.make_async_remote_copy(
                buf.at[yc], buf.at[yc], pl_s.at[row], pl_r.at[row], peer, MESH
            ).start()

    def z_gather(buf, row):
        @pl.loop(1, nz)
        def _(i):
            _, peer = z_peer(i)
            pltpu.make_async_remote_copy(
                buf.at[z], buf.at[z], pl_s.at[row], pl_r.at[row], peer, MESH
            ).start()

    for h in range(HALVES):
        plane_scatter(g1src.at[h], r1[h], h)

    halo_right = pltpu.make_async_remote_copy(kv_hbm.at[0], kvh.at[0], ha_s.at[0], ha_r.at[0], right, MESH)
    halo_left = pltpu.make_async_remote_copy(kv_hbm.at[0], kvh.at[1], ha_s.at[1], ha_r.at[1], left, MESH)
    halo_right.start()
    halo_left.start()

    table = rb_ref[...].astype(F32)
    lane = lax.broadcasted_iota(jnp.int32, table.shape, 2)
    first_block = (2 * (q - 1)).astype(F32)
    picks = [
        jnp.sum(jnp.where(lane == 2 * q + b, table, 0.0), axis=2, keepdims=True) - first_block
        for b in range(2)
    ]
    token = lax.broadcasted_iota(jnp.int32, (KEY_HEADS, TOK), 1)
    second = token >= BLOCK
    listed = [jnp.where(second, picks[1][r], picks[0][r]) for r in range(3)]
    middle = jnp.where(second, 3, 2)
    for kb in range(6):
        block_id = 2 * (q - 1) + kb
        usable = (jnp.abs(middle - kb) <= 1) & (block_id >= 0) & (block_id < 2 * n_seq)
        count = jnp.where(usable, 1.0, 0.0)
        for r in range(3):
            count += jnp.where(listed[r] == float(kb), 1.0, 0.0)
        value = jnp.where(count > 3.5, 2.0, jnp.where(count > 2.5, math.log2(3.0), jnp.where(count > 1.5, 1.0, 0.0)))
        value = jnp.where(count > 0.5, value, -1e30)
        for g in range(KEY_HEADS):
            bias[g, kb : kb + 1, :] = value[g : g + 1, :]
    for g in range(KEY_HEADS):
        bias[g, 6:8, :] = jnp.zeros((2, TOK), F32)

    def owner(k, sub):
        j = lax.rem((k * ch + sub * rows) // BLOCK, 2)
        return jnp.where(j == 0, gb_ref[0, 0], gb_ref[0, 1]) // 2

    for h in range(HALVES):
        all_of(r1[h], plane - 1, pl_r.at[h]).wait()
        r1[h][yc] = g1src[h, yc]
        for sub in range(ch // rows):
            holder = lax.rem(owner(yc, sub), plane)
            part = r1[h][holder]
            r2[h][z, :, sub * rows : (sub + 1) * rows, :] = part[:, sub * rows : (sub + 1) * rows, :]
        z_gather(r2[h], 2 + h)
    for h in range(HALVES):
        all_of(r2[h], nz - 1, pl_r.at[2 + h]).wait()
        for sub in range(ch // rows):
            holder = owner(yc, sub) // plane
            part = r2[h][holder]
            gkv[h, yc, :, sub * rows : (sub + 1) * rows, :] = part[:, sub * rows : (sub + 1) * rows, :]
        plane_gather(gkv.at[h], 4 + h)

    load_q.wait()
    halo_right.wait()
    halo_left.wait()

    def store_dq(g):
        return pltpu.make_async_copy(dqv.at[:, cols(g)], dq_hbm.at[0, :, cols(g)], out_sem.at[g])

    def halo_grad(side, g):
        return pltpu.make_async_remote_copy(
            hgs.at[side, g], hgr.at[1 - side, g], hg_s.at[side, g], hg_r.at[1 - side, g],
            left if side == 0 else right, MESH,
        )

    def one_group(h, gg):
        g = h * PER_HALF + gg

        @pl.when(s < n_sec - 1)
        def _():
            shift(g).wait_recv()

        @pl.when(s == n_sec - 1)
        def _():
            loss_copy(g).wait()

        for part, dst in ((0, kall), (1, vall)):
            col = pl.ds(pl.multiple_of((part * KEY_HEADS + g) * HEAD, HEAD), HEAD)
            dst[0:TOK, :] = kvh[0, :, col]
            dst[TOK : 2 * TOK, :] = kvo[:, col]
            dst[2 * TOK : 3 * TOK, :] = kvh[1, :, col]
            half = plane // 2
            dst[3 * TOK :, :] = gkv[h, part * half : (part + 1) * half, gg].reshape(2 * BLOCK, HEAD)
        kallt[...] = kall[...].T
        acc[...] = jnp.zeros_like(acc)
        bias_row = bias[g]
        bias_two = jnp.concatenate([bias_row, bias_row], axis=1)

        @pl.loop(0, GROUP // 2)
        def _(pair):
            at = pl.multiple_of(g * GROUP_COLS + pair * 2 * HEAD, 2 * HEAD)
            here = pl.multiple_of(pair * 2 * HEAD, 2 * HEAD)
            q_wide = qv[:, pl.ds(at, 2 * HEAD)]
            d_wide = dout[g, :, pl.ds(here, 2 * HEAD)]
            q_rows = jnp.concatenate([q_wide[:, :HEAD], q_wide[:, HEAD:]], axis=0)
            d_rows = jnp.concatenate([d_wide[:, :HEAD], d_wide[:, HEAD:]], axis=0)
            scores = lax.dot_general(
                kall[...], q_rows, (((1,), (1,)), ((), ())), preferred_element_type=F32
            )
            scores = (scores * (SCALE * LOG2E)).reshape(8, BLOCK, 2 * TOK) + bias_two[:, None, :]
            scores = scores.reshape(KEYS, 2 * TOK)
            top = jnp.max(scores, axis=0, keepdims=True)
            weights = jnp.exp2(scores - top)
            total = jnp.sum(weights, axis=0, keepdims=True)
            probs = weights * (1.0 / total)
            grad_probs = lax.dot_general(
                vall[...], d_rows, (((1,), (1,)), ((), ())), preferred_element_type=F32
            )
            delta = jnp.sum(probs * grad_probs, axis=0, keepdims=True)
            grad_scores = (probs * (grad_probs - delta) * SCALE).astype(BF16)
            acc[1] += jnp.dot(probs.astype(BF16), d_rows, preferred_element_type=F32)
            acc[0] += jnp.dot(grad_scores, q_rows, preferred_element_type=F32)
            dq_t = jnp.dot(kallt[...], grad_scores, preferred_element_type=F32)
            dq_two = dq_t.T.astype(BF16)
            dqv[:, pl.ds(at, HEAD)] = dq_two[:TOK]
            dqv[:, pl.ds(pl.multiple_of(at + HEAD, HEAD), HEAD)] = dq_two[TOK:]

        store_dq(g).start()
        hgs[0, g] = acc[:, 0:TOK, :]
        own[g] = acc[:, TOK : 2 * TOK, :]
        hgs[1, g] = acc[:, 2 * TOK : 3 * TOK, :]
        half = plane // 2
        for part in range(2):
            g2src[h, part * half : (part + 1) * half, gg] = acc[part, 3 * TOK :, :].reshape(half, ch, HEAD)
        halo_grad(0, g).start()
        halo_grad(1, g).start()

    for h in range(HALVES):
        all_of(gkv.at[h], plane - 1, pl_r.at[4 + h]).wait()

        @pl.loop(0, PER_HALF)
        def _(gg, h=h):
            one_group(h, gg)

        plane_scatter(g2src.at[h], g2r1.at[h], 6 + h)

    for h in range(HALVES):
        all_of(g2r1.at[h], plane - 1, pl_r.at[6 + h]).wait()
        g2r1[h, yc] = g2src[h, yc]
        total = g2r1[h, 0]
        for k in range(1, plane):
            total += g2r1[h, k]
        g2r2[h, z] = total.astype(BF16)
        z_gather(g2r2.at[h], 8 + h)
    for h in range(HALVES):
        all_of(g2r2.at[h], nz - 1, pl_r.at[8 + h]).wait()
        total = g2r2[h, 0].astype(F32)
        for k in range(1, nz):
            total += g2r2[h, k].astype(F32)
        g2f[h, yc] = total.astype(BF16)
        plane_gather(g2f.at[h], 10 + h)

    for g in range(KEY_HEADS):
        for side in range(2):
            halo_grad(side, g).wait_send()
            halo_grad(side, g).wait_recv()
        own[g] += hgr[0, g] + hgr[1, g]
    for h in range(HALVES):
        all_of(g2f.at[h], plane - 1, pl_r.at[10 + h]).wait()
        half = plane // 2
        for gg in range(PER_HALF):
            g = h * PER_HALF + gg
            for part in range(2):
                sums = g2f[h, part * half : (part + 1) * half, gg].reshape(2 * BLOCK, HEAD).astype(F32)
                for n in range(2):
                    grad = own[g, part, n * BLOCK : (n + 1) * BLOCK, :]
                    for j in range(2):
                        mine = gb_ref[0, j] == 2 * q + n
                        grad += jnp.where(mine, sums[j * BLOCK : (j + 1) * BLOCK], 0.0)
                    col = (part * KEY_HEADS + g) * HEAD
                    dkvv[n * BLOCK : (n + 1) * BLOCK, col : col + HEAD] = grad.astype(BF16)
    store_kv = pltpu.make_async_copy(dkvv, dkv_hbm.at[0], out_sem.at[KEY_HEADS])
    store_kv.start()

    @pl.when(s > 0)
    def _():
        for g in range(KEY_HEADS):
            shift(g).wait_send()

    for h in range(HALVES):
        all_of(g1src.at[h], plane - 1, pl_s.at[h]).wait()
        all_of(r2[h], nz - 1, pl_s.at[2 + h]).wait()
        all_of(gkv.at[h], plane - 1, pl_s.at[4 + h]).wait()
        all_of(g2src.at[h], plane - 1, pl_s.at[6 + h]).wait()
        all_of(g2r2.at[h], nz - 1, pl_s.at[8 + h]).wait()
        all_of(g2f.at[h], plane - 1, pl_s.at[10 + h]).wait()
    for g in range(KEY_HEADS):
        store_dq(g).wait()
    store_kv.wait()


def body(n_sec, plane, nz, queries, packed_key_value, incoming, loss_grad, global_blocks, random_blocks):
    ch = 4 * BLOCK // plane
    table = jnp.transpose(random_blocks[0], (2, 1, 0))
    anywhere = pl.BlockSpec(memory_space=pl.ANY)
    vmem = pltpu.VMEM
    dma = pltpu.SemaphoreType.DMA
    wide = 2 * KEY_HEADS * HEAD
    return pl.pallas_call(
        functools.partial(kernel, n_sec, plane, nz),
        out_shape=(
            jax.ShapeDtypeStruct(queries.shape, BF16),
            jax.ShapeDtypeStruct(packed_key_value.shape, BF16),
        ),
        in_specs=[anywhere] * 4 + [pl.BlockSpec(memory_space=pltpu.SMEM), pl.BlockSpec(memory_space=pltpu.VMEM)],
        out_specs=(anywhere, anywhere),
        scratch_shapes=[
            vmem((TOK, HQ * HEAD), BF16),
            vmem((KEY_HEADS, TOK, GROUP_COLS), BF16),
            vmem((TOK, wide), BF16),
            vmem((2, TOK, wide), BF16),
            vmem((KEY_HEADS, 8, TOK), F32),
            vmem((KEYS, HEAD), BF16),
            vmem((KEYS, HEAD), BF16),
            vmem((HEAD, KEYS), BF16),
            vmem((HALVES, plane, PER_HALF, ch, HEAD), BF16),
            vmem((plane, PER_HALF, ch, HEAD), BF16),
            vmem((plane, PER_HALF, ch, HEAD), BF16),
            vmem((nz, PER_HALF, ch, HEAD), BF16),
            vmem((nz, PER_HALF, ch, HEAD), BF16),
            vmem((HALVES, plane, PER_HALF, ch, HEAD), BF16),
            vmem((2, KEYS, HEAD), F32),
            vmem((KEY_HEADS, 2, TOK, HEAD), F32),
            vmem((2, KEY_HEADS, 2, TOK, HEAD), F32),
            vmem((2, KEY_HEADS, 2, TOK, HEAD), F32),
            vmem((HALVES, plane, PER_HALF, ch, HEAD), F32),
            vmem((HALVES, plane, PER_HALF, ch, HEAD), F32),
            vmem((HALVES, nz, PER_HALF, ch, HEAD), BF16),
            vmem((HALVES, plane, PER_HALF, ch, HEAD), BF16),
            vmem((TOK, HQ * HEAD), BF16),
            vmem((TOK, wide), BF16),
            dma((2,)),
            dma((KEY_HEADS,)),
            dma((KEY_HEADS + 1,)),
            dma((KEY_HEADS,)),
            dma((KEY_HEADS,)),
            dma((2,)),
            dma((2,)),
            dma((2, KEY_HEADS)),
            dma((2, KEY_HEADS)),
            dma((12,)),
            dma((12,)),
        ],
        compiler_params=pltpu.CompilerParams(
            collective_id=0, has_side_effects=True, vmem_limit_bytes=40 * 2**20
        ),
    )(queries, packed_key_value, incoming, loss_grad, global_blocks, table)


def solution(mesh):
    n_sec, n_seq = mesh.shape["section"], mesh.shape["seq"]
    plane = math.isqrt(n_seq)
    in_specs = (
        P("section", "seq", None),
        P("section", "seq", None),
        P("section", "seq", None),
        P("seq", None),
        P("section", None),
        P("section", None, None, None),
    )
    out_specs = (P("section", "seq", None), P("section", "seq", None))
    return jax.shard_map(
        functools.partial(body, n_sec, plane, n_seq // plane),
        mesh=mesh, in_specs=in_specs, out_specs=out_specs, check_vma=False,
    )
```

```python
import functools
import math

import jax
import jax.numpy as jnp
from jax import lax
from jax.experimental import pallas as pl
from jax.experimental.pallas import tpu as pltpu
from jax.sharding import PartitionSpec as P

HQ = 24
KEY_HEADS = 4
HEAD = 128
BLOCK = 64
GROUP = 6
TOK = 128
GROUP_COLS = GROUP * HEAD
KEYS = 3 * TOK + 2 * BLOCK
HALVES = 2
PER_HALF = KEY_HEADS // HALVES
MESH = pl.DeviceIdType.MESH
F32 = jnp.float32
BF16 = jnp.bfloat16
SCALE = 1.0 / math.sqrt(HEAD)
LOG2E = math.log2(math.e)


def kernel(
    n_sec, plane, nz,
    q_hbm, kv_hbm, inc_hbm, loss_hbm, gb_ref, rb_hbm,
    dq_hbm, dkv_hbm,
    rb_ref, qv, dout, kvo, kvh, bias, kall, vall, kallt,
    g1src, r1a, r1b, r2a, r2b, gkv,
    acc, own, hgs, hgr, g2src, g2r1, g2r2, g2f, dqv, dkvv,
    in_sem, loss_sem, out_sem, kv_sem,
    sh_s, sh_r, ha_s, ha_r, hg_s, hg_r, pl_s, pl_r,
):
    n_seq = plane * nz
    r1, r2 = (r1a, r1b), (r2a, r2b)
    ch = PER_HALF * 4 * BLOCK // plane
    rows = min(ch, BLOCK)
    s = lax.axis_index("section")
    q = lax.axis_index("seq")
    z = q // plane
    yc = q % plane
    right = (s, lax.rem(q + 1, n_seq))
    left = (s, lax.rem(q + n_seq - 1, n_seq))
    back = (lax.rem(s + n_sec - 1, n_sec), q)
    ahead = (lax.rem(s + 1, n_sec), q)

    def around(n, visit):
        if n > 2:

            @pl.loop(0, n // 2 - 1)
            def _(t):
                visit(n // 2 - t)
                visit(n // 2 + 1 + t)

        if n > 1:
            visit(1)

    def wrap(at, n):
        return jnp.where(at >= n, at - n, at)

    ny = plane // 4
    y, c, zl = (q // 2) % ny, q % 2, yc // (2 * ny)

    def plane_peers(act):
        def at(off, skip=()):
            row = wrap(y + off, ny) * 2
            for dz, dc in ((1, 1), (1, 0), (0, 1), (0, 0)):
                if (dz, dc) not in skip:
                    k = (1 - zl if dz else zl) * (2 * ny) + row + (1 - c if dc else c)
                    act(k, (s, z * plane + k))

        around(ny, at)
        at(0, ((0, 0),))

    def z_peers(act):
        def at(off):
            k = wrap(z + off, nz)
            act(k, (s, k * plane + yc))

        around(nz, at)

    load_kv = pltpu.make_async_copy(kv_hbm.at[0], kvo, in_sem.at[0])
    load_q = pltpu.make_async_copy(q_hbm.at[0], qv, in_sem.at[1])
    load_rb = pltpu.make_async_copy(rb_hbm, rb_ref, in_sem.at[2])
    load_kv.start()
    load_rb.start()
    load_q.start()

    def cols(g):
        return pl.ds(pl.multiple_of(g * GROUP_COLS, GROUP_COLS), GROUP_COLS)

    def loss_copy(g):
        return pltpu.make_async_copy(loss_hbm.at[:, cols(g)], dout.at[g], loss_sem.at[g])

    @pl.when(s == n_sec - 1)
    def _():
        for g in range(KEY_HEADS):
            loss_copy(g).start()

    barrier = pltpu.get_barrier_semaphore()
    for peer in (right, left, back, ahead):
        pl.semaphore_signal(barrier, inc=1, device_id=peer, device_id_type=MESH)

    def greet(_, peer):
        pl.semaphore_signal(barrier, inc=1, device_id=peer, device_id_type=MESH)

    plane_peers(greet)
    z_peers(greet)

    load_kv.wait()
    for j in range(2):
        high = lax.rem(gb_ref[0, j], 2) == 1
        block = jnp.where(high, kvo[BLOCK:, :], kvo[:BLOCK, :])
        for part in range(2):
            for g in range(KEY_HEADS):
                col = part * KEY_HEADS * HEAD + g * HEAD
                for i in range(BLOCK // rows):
                    at = ((g % PER_HALF) * 4 + part * 2 + j) * BLOCK + i * rows
                    g1src[g // PER_HALF, at // ch, at % ch : at % ch + rows, :] = block[
                        i * rows : (i + 1) * rows, col : col + HEAD
                    ]

    pl.semaphore_wait(barrier, 4 + plane - 1 + nz - 1)

    def shift(g):
        return pltpu.make_async_remote_copy(
            inc_hbm.at[0, :, cols(g)], dout.at[g], sh_s.at[g], sh_r.at[g], back, MESH
        )

    def all_of(buf, count, sem):
        return pltpu.make_async_copy(buf.at[pl.ds(0, count)], buf.at[pl.ds(0, count)], sem)

    def plane_scatter(src, dst, row):
        def send(k, peer):
            pltpu.make_async_remote_copy(
                src.at[k], dst.at[yc], pl_s.at[row], pl_r.at[row], peer, MESH
            ).start()

        plane_peers(send)

    def plane_gather(buf, row):
        def send(_, peer):
            pltpu.make_async_remote_copy(
                buf.at[yc], buf.at[yc], pl_s.at[row], pl_r.at[row], peer, MESH
            ).start()

        plane_peers(send)

    def z_gather(buf, row):
        def send(_, peer):
            pltpu.make_async_remote_copy(
                buf.at[z], buf.at[z], pl_s.at[row], pl_r.at[row], peer, MESH
            ).start()

        z_peers(send)

    @pl.when(s > 0)
    def _():
        for g in range(KEY_HEADS):
            shift(g).start()

    for h in range(HALVES):
        plane_scatter(g1src.at[h], r1[h], h)

    halo_right = pltpu.make_async_remote_copy(kv_hbm.at[0], kvh.at[0], ha_s.at[0], ha_r.at[0], right, MESH)
    halo_left = pltpu.make_async_remote_copy(kv_hbm.at[0], kvh.at[1], ha_s.at[1], ha_r.at[1], left, MESH)

    load_rb.wait()
    table = rb_ref[...].astype(F32)
    lane = lax.broadcasted_iota(jnp.int32, table.shape, 2)
    first_block = (2 * (q - 1)).astype(F32)
    picks = [
        jnp.sum(jnp.where(lane == 2 * q + b, table, 0.0), axis=2, keepdims=True) - first_block
        for b in range(2)
    ]
    token = lax.broadcasted_iota(jnp.int32, (KEY_HEADS, TOK), 1)
    second = token >= BLOCK
    listed = [jnp.where(second, picks[1][r], picks[0][r]) for r in range(3)]
    middle = jnp.where(second, 3, 2)
    for kb in range(6):
        block_id = 2 * (q - 1) + kb
        usable = (jnp.abs(middle - kb) <= 1) & (block_id >= 0) & (block_id < 2 * n_seq)
        count = jnp.where(usable, 1.0, 0.0)
        for r in range(3):
            count += jnp.where(listed[r] == float(kb), 1.0, 0.0)
        value = jnp.where(count > 3.5, 2.0, jnp.where(count > 2.5, math.log2(3.0), jnp.where(count > 1.5, 1.0, 0.0)))
        value = jnp.where(count > 0.5, value, -1e30)
        for g in range(KEY_HEADS):
            bias[g, kb : kb + 1, :] = value[g : g + 1, :]
    for g in range(KEY_HEADS):
        bias[g, 6:8, :] = jnp.zeros((2, TOK), F32)

    def owner(k, sub):
        j = lax.rem((k * ch + sub * rows) // BLOCK, 2)
        return jnp.where(j == 0, gb_ref[0, 0], gb_ref[0, 1]) // 2

    for h in range(HALVES):
        all_of(r1[h], plane - 1, pl_r.at[h]).wait()
        r1[h][yc] = g1src[h, yc]
        for sub in range(ch // rows):
            holder = lax.rem(owner(yc, sub), plane)
            part = r1[h][holder]
            r2[h][z, sub * rows : (sub + 1) * rows, :] = part[sub * rows : (sub + 1) * rows, :]
        z_gather(r2[h], 2 + h)
    halo_right.start()
    halo_left.start()
    for h in range(HALVES):
        all_of(r2[h], nz - 1, pl_r.at[2 + h]).wait()
        for sub in range(ch // rows):
            holder = owner(yc, sub) // plane
            part = r2[h][holder]
            gkv[h, yc, sub * rows : (sub + 1) * rows, :] = part[sub * rows : (sub + 1) * rows, :]
        plane_gather(gkv.at[h], 4 + h)

    load_q.wait()
    halo_right.wait()
    halo_left.wait()

    def store_dq(g):
        return pltpu.make_async_copy(dqv.at[:, cols(g)], dq_hbm.at[0, :, cols(g)], out_sem.at[g])

    def halo_grad(side, g):
        return pltpu.make_async_remote_copy(
            hgs.at[side, g], hgr.at[1 - side, g], hg_s.at[side, g], hg_r.at[1 - side, g],
            left if side == 0 else right, MESH,
        )

    def quarter(gg, part):
        return pl.ds((2 * gg + part) * (plane // 4), plane // 4)

    def one_group(h, gg):
        g = h * PER_HALF + gg

        @pl.when(s < n_sec - 1)
        def _():
            shift(g).wait_recv()

        @pl.when(s == n_sec - 1)
        def _():
            loss_copy(g).wait()

        for part, dst in ((0, kall), (1, vall)):
            col = pl.ds(pl.multiple_of((part * KEY_HEADS + g) * HEAD, HEAD), HEAD)
            dst[0:TOK, :] = kvh[0, :, col]
            dst[TOK : 2 * TOK, :] = kvo[:, col]
            dst[2 * TOK : 3 * TOK, :] = kvh[1, :, col]
            dst[3 * TOK :, :] = gkv[h, quarter(gg, part)].reshape(2 * BLOCK, HEAD)
        kallt[...] = kall[...].T
        acc[...] = jnp.zeros_like(acc)
        bias_row = bias[g]
        bias_two = jnp.concatenate([bias_row, bias_row], axis=1)

        @pl.loop(0, GROUP // 2)
        def _(pair):
            at = pl.multiple_of(g * GROUP_COLS + pair * 2 * HEAD, 2 * HEAD)
            here = pl.multiple_of(pair * 2 * HEAD, 2 * HEAD)
            q_wide = qv[:, pl.ds(at, 2 * HEAD)]
            d_wide = dout[g, :, pl.ds(here, 2 * HEAD)]
            q_rows = jnp.concatenate([q_wide[:, :HEAD], q_wide[:, HEAD:]], axis=0)
            d_rows = jnp.concatenate([d_wide[:, :HEAD], d_wide[:, HEAD:]], axis=0)
            scores = lax.dot_general(
                kall[...], q_rows, (((1,), (1,)), ((), ())), preferred_element_type=F32
            )
            scores = (scores * (SCALE * LOG2E)).reshape(8, BLOCK, 2 * TOK) + bias_two[:, None, :]
            scores = scores.reshape(KEYS, 2 * TOK)
            top = jnp.max(scores, axis=0, keepdims=True)
            weights = jnp.exp2(scores - top)
            total = jnp.sum(weights, axis=0, keepdims=True)
            probs = weights * (1.0 / total)
            grad_probs = lax.dot_general(
                vall[...], d_rows, (((1,), (1,)), ((), ())), preferred_element_type=F32
            )
            delta = jnp.sum(probs * grad_probs, axis=0, keepdims=True)
            grad_scores = (probs * (grad_probs - delta) * SCALE).astype(BF16)
            acc[1] += jnp.dot(probs.astype(BF16), d_rows, preferred_element_type=F32)
            acc[0] += jnp.dot(grad_scores, q_rows, preferred_element_type=F32)
            dq_t = jnp.dot(kallt[...], grad_scores, preferred_element_type=F32)
            dq_two = dq_t.T.astype(BF16)
            dqv[:, pl.ds(at, HEAD)] = dq_two[:TOK]
            dqv[:, pl.ds(pl.multiple_of(at + HEAD, HEAD), HEAD)] = dq_two[TOK:]

        store_dq(g).start()
        hgs[0, g] = acc[:, 0:TOK, :]
        own[g] = acc[:, TOK : 2 * TOK, :]
        hgs[1, g] = acc[:, 2 * TOK : 3 * TOK, :]
        for part in range(2):
            sums = acc[part, 3 * TOK :, :].astype(BF16)
            g2src[h, quarter(gg, part)] = sums.reshape(plane // 4, ch, HEAD)

    for h in range(HALVES):
        all_of(gkv.at[h], plane - 1, pl_r.at[4 + h]).wait()

        @pl.loop(0, PER_HALF)
        def _(gg, h=h):
            one_group(h, gg)

        plane_scatter(g2src.at[h], g2r1.at[h], 6 + h)
        for g in range(h * PER_HALF, (h + 1) * PER_HALF):
            halo_grad(0, g).start()
            halo_grad(1, g).start()

    for h in range(HALVES):
        all_of(g2r1.at[h], plane - 1, pl_r.at[6 + h]).wait()
        g2r1[h, yc] = g2src[h, yc]
        total = jnp.sum(g2r1[h].astype(F32), axis=0)
        g2r2[h, z] = total.astype(BF16)
        z_gather(g2r2.at[h], 8 + h)
    for h in range(HALVES):
        all_of(g2r2.at[h], nz - 1, pl_r.at[8 + h]).wait()
        total = jnp.sum(g2r2[h].astype(F32), axis=0)
        g2f[h, yc] = total.astype(BF16)
        plane_gather(g2f.at[h], 10 + h)

    def store_kv(h, part):
        at = pl.ds((part * KEY_HEADS + h * PER_HALF) * HEAD, PER_HALF * HEAD)
        return pltpu.make_async_copy(dkvv.at[:, at], dkv_hbm.at[0, :, at], kv_sem.at[h, part])

    for g in range(KEY_HEADS):
        for side in range(2):
            halo_grad(side, g).wait_send()
            halo_grad(side, g).wait_recv()
        own[g] += hgr[0, g] + hgr[1, g]
    for h in range(HALVES):
        all_of(g2f.at[h], plane - 1, pl_r.at[10 + h]).wait()
        for gg in range(PER_HALF):
            g = h * PER_HALF + gg
            for part in range(2):
                sums = g2f[h, quarter(gg, part)].reshape(2 * BLOCK, HEAD).astype(F32)
                for n in range(2):
                    grad = own[g, part, n * BLOCK : (n + 1) * BLOCK, :]
                    for j in range(2):
                        mine = gb_ref[0, j] == 2 * q + n
                        grad += jnp.where(mine, sums[j * BLOCK : (j + 1) * BLOCK], 0.0)
                    col = (part * KEY_HEADS + g) * HEAD
                    dkvv[n * BLOCK : (n + 1) * BLOCK, col : col + HEAD] = grad.astype(BF16)
        for part in range(2):
            store_kv(h, part).start()

    @pl.when(s > 0)
    def _():
        for g in range(KEY_HEADS):
            shift(g).wait_send()

    for h in range(HALVES):
        all_of(g1src.at[h], plane - 1, pl_s.at[h]).wait()
        all_of(r2[h], nz - 1, pl_s.at[2 + h]).wait()
        all_of(gkv.at[h], plane - 1, pl_s.at[4 + h]).wait()
        all_of(g2src.at[h], plane - 1, pl_s.at[6 + h]).wait()
        all_of(g2r2.at[h], nz - 1, pl_s.at[8 + h]).wait()
        all_of(g2f.at[h], plane - 1, pl_s.at[10 + h]).wait()
    for g in range(KEY_HEADS):
        store_dq(g).wait()
    for h in range(HALVES):
        for part in range(2):
            store_kv(h, part).wait()


def body(n_sec, plane, nz, queries, packed_key_value, incoming, loss_grad, global_blocks, random_blocks):
    ch = PER_HALF * 4 * BLOCK // plane
    table = jnp.transpose(random_blocks[0], (2, 1, 0))
    anywhere = pl.BlockSpec(memory_space=pl.ANY)
    vmem = pltpu.VMEM
    dma = pltpu.SemaphoreType.DMA
    wide = 2 * KEY_HEADS * HEAD
    return pl.pallas_call(
        functools.partial(kernel, n_sec, plane, nz),
        out_shape=(
            jax.ShapeDtypeStruct(queries.shape, BF16),
            jax.ShapeDtypeStruct(packed_key_value.shape, BF16),
        ),
        in_specs=[anywhere] * 4 + [pl.BlockSpec(memory_space=pltpu.SMEM), anywhere],
        out_specs=(anywhere, anywhere),
        scratch_shapes=[
            vmem(table.shape, jnp.int32),
            vmem((TOK, HQ * HEAD), BF16),
            vmem((KEY_HEADS, TOK, GROUP_COLS), BF16),
            vmem((TOK, wide), BF16),
            vmem((2, TOK, wide), BF16),
            vmem((KEY_HEADS, 8, TOK), F32),
            vmem((KEYS, HEAD), BF16),
            vmem((KEYS, HEAD), BF16),
            vmem((HEAD, KEYS), BF16),
            vmem((HALVES, plane, ch, HEAD), BF16),
            vmem((plane, ch, HEAD), BF16),
            vmem((plane, ch, HEAD), BF16),
            vmem((nz, ch, HEAD), BF16),
            vmem((nz, ch, HEAD), BF16),
            vmem((HALVES, plane, ch, HEAD), BF16),
            vmem((2, KEYS, HEAD), F32),
            vmem((KEY_HEADS, 2, TOK, HEAD), F32),
            vmem((2, KEY_HEADS, 2, TOK, HEAD), F32),
            vmem((2, KEY_HEADS, 2, TOK, HEAD), F32),
            vmem((HALVES, plane, ch, HEAD), BF16),
            vmem((HALVES, plane, ch, HEAD), BF16),
            vmem((HALVES, nz, ch, HEAD), BF16),
            vmem((HALVES, plane, ch, HEAD), BF16),
            vmem((TOK, HQ * HEAD), BF16),
            vmem((TOK, wide), BF16),
            dma((3,)),
            dma((KEY_HEADS,)),
            dma((KEY_HEADS,)),
            dma((HALVES, 2)),
            dma((KEY_HEADS,)),
            dma((KEY_HEADS,)),
            dma((2,)),
            dma((2,)),
            dma((2, KEY_HEADS)),
            dma((2, KEY_HEADS)),
            dma((12,)),
            dma((12,)),
        ],
        compiler_params=pltpu.CompilerParams(
            collective_id=0, has_side_effects=True, vmem_limit_bytes=60 * 2**20
        ),
    )(queries, packed_key_value, incoming, loss_grad, global_blocks, table)


def solution(mesh):
    n_sec, n_seq = mesh.shape["section"], mesh.shape["seq"]
    plane = 2 * math.isqrt(n_seq)
    in_specs = (
        P("section", "seq", None),
        P("section", "seq", None),
        P("section", "seq", None),
        P("seq", None),
        P("section", None),
        P("section", None, None, None),
    )
    out_specs = (P("section", "seq", None), P("section", "seq", None))
    return jax.shard_map(
        functools.partial(body, n_sec, plane, n_seq // plane),
        mesh=mesh, in_specs=in_specs, out_specs=out_specs, check_vma=False,
    )
```

```python
import functools
import math

import jax
import jax.numpy as jnp
from jax import lax
from jax.experimental import pallas as pl
from jax.experimental.pallas import tpu as pltpu
from jax.sharding import PartitionSpec as P

HQ = 24
KEY_HEADS = 4
HEAD = 128
BLOCK = 64
GROUP = 6
TOK = 128
GROUP_COLS = GROUP * HEAD
KEYS = 3 * TOK + 2 * BLOCK
HALVES = 2
PER_HALF = KEY_HEADS // HALVES
MESH = pl.DeviceIdType.MESH
F32 = jnp.float32
BF16 = jnp.bfloat16
SCALE = 1.0 / math.sqrt(HEAD)
LOG2E = math.log2(math.e)


def kernel(
    n_sec, plane, nz,
    q_hbm, kv_hbm, inc_hbm, loss_hbm, gb_ref, rb_hbm,
    dq_hbm, dkv_hbm,
    rb_ref, qv, dout, kvo, kvh, bias, kall, vall, kallt,
    g1src, r1a, r1b, r2a, r2b, gkv,
    acc, own, hgs, hgr, g2src, g2r1, g2r2, g2f, dqv, dkvv,
    in_sem, loss_sem, out_sem, kv_sem,
    sh_s, sh_r, ha_s, ha_r, hg_s, hg_r, pl_s, pl_r,
):
    n_seq = plane * nz
    r1, r2 = (r1a, r1b), (r2a, r2b)
    ch = PER_HALF * 4 * BLOCK // plane
    rows = min(ch, BLOCK)
    s = lax.axis_index("section")
    q = lax.axis_index("seq")
    z = q // plane
    yc = q % plane
    right = (s, lax.rem(q + 1, n_seq))
    left = (s, lax.rem(q + n_seq - 1, n_seq))
    back = (lax.rem(s + n_sec - 1, n_sec), q)
    ahead = (lax.rem(s + 1, n_sec), q)

    def around(n, visit):
        if n > 2:

            @pl.loop(0, n // 2 - 1)
            def _(t):
                visit(n // 2 - t)
                visit(n // 2 + 1 + t)

        if n > 1:
            visit(1)

    def wrap(at, n):
        return jnp.where(at >= n, at - n, at)

    ny = plane // 4
    y, c, zl = (q // 2) % ny, q % 2, yc // (2 * ny)

    def plane_peers(act):
        def at(off, skip=()):
            row = wrap(y + off, ny) * 2
            for dz, dc in ((1, 1), (1, 0), (0, 1), (0, 0)):
                if (dz, dc) not in skip:
                    k = (1 - zl if dz else zl) * (2 * ny) + row + (1 - c if dc else c)
                    act(k, (s, z * plane + k))

        around(ny, at)
        at(0, ((0, 0),))

    def z_peers(act):
        def at(off):
            k = wrap(z + off, nz)
            act(k, (s, k * plane + yc))

        around(nz, at)

    load_kv = pltpu.make_async_copy(kv_hbm.at[0], kvo, in_sem.at[0])
    load_q = pltpu.make_async_copy(q_hbm.at[0], qv, in_sem.at[1])
    load_rb = pltpu.make_async_copy(rb_hbm, rb_ref, in_sem.at[2])
    load_kv.start()
    load_rb.start()
    load_q.start()

    def cols(g):
        return pl.ds(pl.multiple_of(g * GROUP_COLS, GROUP_COLS), GROUP_COLS)

    def loss_copy(g):
        return pltpu.make_async_copy(loss_hbm.at[:, cols(g)], dout.at[g], loss_sem.at[g])

    @pl.when(s == n_sec - 1)
    def _():
        for g in range(KEY_HEADS):
            loss_copy(g).start()

    barrier = pltpu.get_barrier_semaphore()
    def greet(_, peer):
        pl.semaphore_signal(barrier, inc=1, device_id=peer, device_id_type=MESH)

    z_peers(greet)
    plane_peers(greet)
    for peer in (right, left, back, ahead):
        greet(0, peer)

    load_kv.wait()
    for j in range(2):
        high = lax.rem(gb_ref[0, j], 2) == 1
        block = jnp.where(high, kvo[BLOCK:, :], kvo[:BLOCK, :])
        for part in range(2):
            for g in range(KEY_HEADS):
                col = part * KEY_HEADS * HEAD + g * HEAD
                for i in range(BLOCK // rows):
                    at = ((g % PER_HALF) * 4 + part * 2 + j) * BLOCK + i * rows
                    g1src[g // PER_HALF, at // ch, at % ch : at % ch + rows, :] = block[
                        i * rows : (i + 1) * rows, col : col + HEAD
                    ]

    pl.semaphore_wait(barrier, 4 + plane - 1 + nz - 1)

    def shift(g):
        return pltpu.make_async_remote_copy(
            inc_hbm.at[0, :, cols(g)], dout.at[g], sh_s.at[g], sh_r.at[g], back, MESH
        )

    def all_of(buf, count, sem):
        return pltpu.make_async_copy(buf.at[pl.ds(0, count)], buf.at[pl.ds(0, count)], sem)

    def plane_scatter(src, dst, row):
        def send(k, peer):
            pltpu.make_async_remote_copy(
                src.at[k], dst.at[yc], pl_s.at[row], pl_r.at[row], peer, MESH
            ).start()

        plane_peers(send)

    def plane_gather(buf, row):
        def send(_, peer):
            pltpu.make_async_remote_copy(
                buf.at[yc], buf.at[yc], pl_s.at[row], pl_r.at[row], peer, MESH
            ).start()

        plane_peers(send)

    def z_gather(buf, row):
        def send(_, peer):
            pltpu.make_async_remote_copy(
                buf.at[z], buf.at[z], pl_s.at[row], pl_r.at[row], peer, MESH
            ).start()

        z_peers(send)

    @pl.when(s > 0)
    def _():
        for g in range(KEY_HEADS):
            shift(g).start()

    for h in range(HALVES):
        plane_scatter(g1src.at[h], r1[h], h)

    halo_right = pltpu.make_async_remote_copy(kv_hbm.at[0], kvh.at[0], ha_s.at[0], ha_r.at[0], right, MESH)
    halo_left = pltpu.make_async_remote_copy(kv_hbm.at[0], kvh.at[1], ha_s.at[1], ha_r.at[1], left, MESH)

    load_rb.wait()
    table = rb_ref[...].astype(F32)
    lane = lax.broadcasted_iota(jnp.int32, table.shape, 2)
    first_block = (2 * (q - 1)).astype(F32)
    picks = [
        jnp.sum(jnp.where(lane == 2 * q + b, table, 0.0), axis=2, keepdims=True) - first_block
        for b in range(2)
    ]
    token = lax.broadcasted_iota(jnp.int32, (KEY_HEADS, TOK), 1)
    second = token >= BLOCK
    listed = [jnp.where(second, picks[1][r], picks[0][r]) for r in range(3)]
    middle = jnp.where(second, 3, 2)
    for kb in range(6):
        block_id = 2 * (q - 1) + kb
        usable = (jnp.abs(middle - kb) <= 1) & (block_id >= 0) & (block_id < 2 * n_seq)
        count = jnp.where(usable, 1.0, 0.0)
        for r in range(3):
            count += jnp.where(listed[r] == float(kb), 1.0, 0.0)
        value = jnp.where(count > 3.5, 2.0, jnp.where(count > 2.5, math.log2(3.0), jnp.where(count > 1.5, 1.0, 0.0)))
        value = jnp.where(count > 0.5, value, -1e30)
        for g in range(KEY_HEADS):
            bias[g, kb : kb + 1, :] = value[g : g + 1, :]
    for g in range(KEY_HEADS):
        bias[g, 6:8, :] = jnp.zeros((2, TOK), F32)

    def owner(k, sub):
        j = lax.rem((k * ch + sub * rows) // BLOCK, 2)
        return jnp.where(j == 0, gb_ref[0, 0], gb_ref[0, 1]) // 2

    for h in range(HALVES):
        all_of(r1[h], plane - 1, pl_r.at[h]).wait()
        r1[h][yc] = g1src[h, yc]
        for sub in range(ch // rows):
            holder = lax.rem(owner(yc, sub), plane)
            part = r1[h][holder]
            r2[h][z, sub * rows : (sub + 1) * rows, :] = part[sub * rows : (sub + 1) * rows, :]
        z_gather(r2[h], 2 + h)
    halo_right.start()
    halo_left.start()
    for h in range(HALVES):
        all_of(r2[h], nz - 1, pl_r.at[2 + h]).wait()
        for sub in range(ch // rows):
            holder = owner(yc, sub) // plane
            part = r2[h][holder]
            gkv[h, yc, sub * rows : (sub + 1) * rows, :] = part[sub * rows : (sub + 1) * rows, :]
        plane_gather(gkv.at[h], 4 + h)

    load_q.wait()
    halo_right.wait()
    halo_left.wait()

    def store_dq(g):
        return pltpu.make_async_copy(dqv.at[:, cols(g)], dq_hbm.at[0, :, cols(g)], out_sem.at[g])

    def halo_grad(side, g):
        return pltpu.make_async_remote_copy(
            hgs.at[side, g], hgr.at[1 - side, g], hg_s.at[side, g], hg_r.at[1 - side, g],
            left if side == 0 else right, MESH,
        )

    def quarter(gg, part):
        return pl.ds((2 * gg + part) * (plane // 4), plane // 4)

    def one_group(h, gg):
        g = h * PER_HALF + gg

        @pl.when(s < n_sec - 1)
        def _():
            shift(g).wait_recv()

        @pl.when(s == n_sec - 1)
        def _():
            loss_copy(g).wait()

        for part, dst in ((0, kall), (1, vall)):
            col = pl.ds(pl.multiple_of((part * KEY_HEADS + g) * HEAD, HEAD), HEAD)
            dst[0:TOK, :] = kvh[0, :, col]
            dst[TOK : 2 * TOK, :] = kvo[:, col]
            dst[2 * TOK : 3 * TOK, :] = kvh[1, :, col]
            dst[3 * TOK :, :] = gkv[h, quarter(gg, part)].reshape(2 * BLOCK, HEAD)
        kallt[...] = kall[...].T
        acc[...] = jnp.zeros_like(acc)
        bias_row = bias[g]
        bias_two = jnp.concatenate([bias_row, bias_row], axis=1)

        @pl.loop(0, GROUP // 2)
        def _(pair):
            at = pl.multiple_of(g * GROUP_COLS + pair * 2 * HEAD, 2 * HEAD)
            here = pl.multiple_of(pair * 2 * HEAD, 2 * HEAD)
            q_wide = qv[:, pl.ds(at, 2 * HEAD)]
            d_wide = dout[g, :, pl.ds(here, 2 * HEAD)]
            q_rows = jnp.concatenate([q_wide[:, :HEAD], q_wide[:, HEAD:]], axis=0)
            d_rows = jnp.concatenate([d_wide[:, :HEAD], d_wide[:, HEAD:]], axis=0)
            scores = lax.dot_general(
                kall[...], q_rows, (((1,), (1,)), ((), ())), preferred_element_type=F32
            )
            scores = (scores * (SCALE * LOG2E)).reshape(8, BLOCK, 2 * TOK) + bias_two[:, None, :]
            scores = scores.reshape(KEYS, 2 * TOK)
            top = jnp.max(scores, axis=0, keepdims=True)
            weights = jnp.exp2(scores - top)
            total = jnp.sum(weights, axis=0, keepdims=True)
            probs = weights * (1.0 / total)
            grad_probs = lax.dot_general(
                vall[...], d_rows, (((1,), (1,)), ((), ())), preferred_element_type=F32
            )
            delta = jnp.sum(probs * grad_probs, axis=0, keepdims=True)
            grad_scores = (probs * (grad_probs - delta) * SCALE).astype(BF16)
            acc[1] += jnp.dot(probs.astype(BF16), d_rows, preferred_element_type=F32)
            acc[0] += jnp.dot(grad_scores, q_rows, preferred_element_type=F32)
            dq_t = jnp.dot(kallt[...], grad_scores, preferred_element_type=F32)
            dq_two = dq_t.T.astype(BF16)
            dqv[:, pl.ds(at, HEAD)] = dq_two[:TOK]
            dqv[:, pl.ds(pl.multiple_of(at + HEAD, HEAD), HEAD)] = dq_two[TOK:]

        store_dq(g).start()
        hgs[0, g] = acc[:, 0:TOK, :].astype(BF16)
        own[g] = acc[:, TOK : 2 * TOK, :]
        hgs[1, g] = acc[:, 2 * TOK : 3 * TOK, :].astype(BF16)
        for part in range(2):
            sums = acc[part, 3 * TOK :, :].astype(BF16)
            g2src[h, quarter(gg, part)] = sums.reshape(plane // 4, ch, HEAD)

    for h in range(HALVES):
        all_of(gkv.at[h], plane - 1, pl_r.at[4 + h]).wait()

        @pl.loop(0, PER_HALF)
        def _(gg, h=h):
            one_group(h, gg)

        plane_scatter(g2src.at[h], g2r1.at[h], 6 + h)
        for g in range(h * PER_HALF, (h + 1) * PER_HALF):
            halo_grad(0, g).start()
            halo_grad(1, g).start()

    for h in range(HALVES):
        all_of(g2r1.at[h], plane - 1, pl_r.at[6 + h]).wait()
        g2r1[h, yc] = g2src[h, yc]
        total = jnp.sum(g2r1[h].astype(F32), axis=0)
        g2r2[h, z] = total.astype(BF16)
        z_gather(g2r2.at[h], 8 + h)
    for h in range(HALVES):
        all_of(g2r2.at[h], nz - 1, pl_r.at[8 + h]).wait()
        total = jnp.sum(g2r2[h].astype(F32), axis=0)
        g2f[h, yc] = total.astype(BF16)
        plane_gather(g2f.at[h], 10 + h)

    def store_kv(h, part):
        at = pl.ds((part * KEY_HEADS + h * PER_HALF) * HEAD, PER_HALF * HEAD)
        return pltpu.make_async_copy(dkvv.at[:, at], dkv_hbm.at[0, :, at], kv_sem.at[h, part])

    for g in range(KEY_HEADS):
        for side in range(2):
            halo_grad(side, g).wait_send()
            halo_grad(side, g).wait_recv()
        own[g] += hgr[0, g].astype(F32) + hgr[1, g].astype(F32)
    for h in range(HALVES):
        all_of(g2f.at[h], plane - 1, pl_r.at[10 + h]).wait()
        for gg in range(PER_HALF):
            g = h * PER_HALF + gg
            for part in range(2):
                sums = g2f[h, quarter(gg, part)].reshape(2 * BLOCK, HEAD).astype(F32)
                for n in range(2):
                    grad = own[g, part, n * BLOCK : (n + 1) * BLOCK, :]
                    for j in range(2):
                        mine = gb_ref[0, j] == 2 * q + n
                        grad += jnp.where(mine, sums[j * BLOCK : (j + 1) * BLOCK], 0.0)
                    col = (part * KEY_HEADS + g) * HEAD
                    dkvv[n * BLOCK : (n + 1) * BLOCK, col : col + HEAD] = grad.astype(BF16)
        for part in range(2):
            store_kv(h, part).start()

    @pl.when(s > 0)
    def _():
        for g in range(KEY_HEADS):
            shift(g).wait_send()

    for h in range(HALVES):
        all_of(g1src.at[h], plane - 1, pl_s.at[h]).wait()
        all_of(r2[h], nz - 1, pl_s.at[2 + h]).wait()
        all_of(gkv.at[h], plane - 1, pl_s.at[4 + h]).wait()
        all_of(g2src.at[h], plane - 1, pl_s.at[6 + h]).wait()
        all_of(g2r2.at[h], nz - 1, pl_s.at[8 + h]).wait()
        all_of(g2f.at[h], plane - 1, pl_s.at[10 + h]).wait()
    for g in range(KEY_HEADS):
        store_dq(g).wait()
    for h in range(HALVES):
        for part in range(2):
            store_kv(h, part).wait()


def body(n_sec, plane, nz, queries, packed_key_value, incoming, loss_grad, global_blocks, random_blocks):
    ch = PER_HALF * 4 * BLOCK // plane
    table = jnp.transpose(random_blocks[0], (2, 1, 0))
    anywhere = pl.BlockSpec(memory_space=pl.ANY)
    vmem = pltpu.VMEM
    dma = pltpu.SemaphoreType.DMA
    wide = 2 * KEY_HEADS * HEAD
    return pl.pallas_call(
        functools.partial(kernel, n_sec, plane, nz),
        out_shape=(
            jax.ShapeDtypeStruct(queries.shape, BF16),
            jax.ShapeDtypeStruct(packed_key_value.shape, BF16),
        ),
        in_specs=[anywhere] * 4 + [pl.BlockSpec(memory_space=pltpu.SMEM), anywhere],
        out_specs=(anywhere, anywhere),
        scratch_shapes=[
            vmem(table.shape, jnp.int32),
            vmem((TOK, HQ * HEAD), BF16),
            vmem((KEY_HEADS, TOK, GROUP_COLS), BF16),
            vmem((TOK, wide), BF16),
            vmem((2, TOK, wide), BF16),
            vmem((KEY_HEADS, 8, TOK), F32),
            vmem((KEYS, HEAD), BF16),
            vmem((KEYS, HEAD), BF16),
            vmem((HEAD, KEYS), BF16),
            vmem((HALVES, plane, ch, HEAD), BF16),
            vmem((plane, ch, HEAD), BF16),
            vmem((plane, ch, HEAD), BF16),
            vmem((nz, ch, HEAD), BF16),
            vmem((nz, ch, HEAD), BF16),
            vmem((HALVES, plane, ch, HEAD), BF16),
            vmem((2, KEYS, HEAD), F32),
            vmem((KEY_HEADS, 2, TOK, HEAD), F32),
            vmem((2, KEY_HEADS, 2, TOK, HEAD), BF16),
            vmem((2, KEY_HEADS, 2, TOK, HEAD), BF16),
            vmem((HALVES, plane, ch, HEAD), BF16),
            vmem((HALVES, plane, ch, HEAD), BF16),
            vmem((HALVES, nz, ch, HEAD), BF16),
            vmem((HALVES, plane, ch, HEAD), BF16),
            vmem((TOK, HQ * HEAD), BF16),
            vmem((TOK, wide), BF16),
            dma((3,)),
            dma((KEY_HEADS,)),
            dma((KEY_HEADS,)),
            dma((HALVES, 2)),
            dma((KEY_HEADS,)),
            dma((KEY_HEADS,)),
            dma((2,)),
            dma((2,)),
            dma((2, KEY_HEADS)),
            dma((2, KEY_HEADS)),
            dma((12,)),
            dma((12,)),
        ],
        compiler_params=pltpu.CompilerParams(
            collective_id=0, has_side_effects=True, vmem_limit_bytes=60 * 2**20
        ),
    )(queries, packed_key_value, incoming, loss_grad, global_blocks, table)


def solution(mesh):
    n_sec, n_seq = mesh.shape["section"], mesh.shape["seq"]
    plane = 2 * math.isqrt(n_seq)
    in_specs = (
        P("section", "seq", None),
        P("section", "seq", None),
        P("section", "seq", None),
        P("seq", None),
        P("section", None),
        P("section", None, None, None),
    )
    out_specs = (P("section", "seq", None), P("section", "seq", None))
    return jax.shard_map(
        functools.partial(body, n_sec, plane, n_seq // plane),
        mesh=mesh, in_specs=in_specs, out_specs=out_specs, check_vma=False,
    )
```
